32 devices in a mesh: lat: 4 (over x, core), lon: 8 (over z, y).
Axes of the slice: x: 2, y: 2, z: 4, core: 2. Of those that a mesh axis runs over, the one named last changes fastest.
Arguments:
- initial_state: float32 [4, 8, 64, 256], P('lat', 'lon'), may hold values from -6 to 6
- initial_reservoir: bfloat16 [4, 8, 64, 2048], P('lat', 'lon'), may hold values from -0.8984375 to 0.8984375
- coupling: bfloat16 [4, 8, 16, 4, 128, 128], P('lat', 'lon'), may hold values from -0.1875 to 0.1875
- input_weight: bfloat16 [4, 8, 16, 128, 128], P('lat', 'lon'), may hold values from -0.5 to 0.5
- readout: bfloat16 [4, 8, 2048, 256], P('lat', 'lon'), may hold values from -0.125 to 0.125
- intersection: int32 [4, 8, 2, 4], P('lat', 'lon'), may hold values from -1 to 7, as said below
Outputs:
- forecast: float32 [8, 4, 8, 64, 256], P(None, 'lat', 'lon')
The draws below stay inside these ranges and needn't reach their ends.
Inputs may be any that keep to these rules, and one draw needn't show every extreme that they name: `intersection`: each list holds distinct point numbers in its first slots and -1 in the rest, with one or more live slots; the north lists of band 0 and the south lists of the last band hold only -1; in longitude sector 0 every list that is not a polar one has all four slots live.
All inputs are finite; a program needn't handle non-finite values.
Results may differ from the reference program's by a relative error of at most 0.018.
Values may be sent and summed in bfloat16 or wider, within the bound.
A program may use at most 64 MiB of HBM per device.

```python
import jax
import jax.numpy as jnp
import numpy as np
from jax import lax

N_RES = 2048
VARS = 32
BLOCK = 128
NCON = 4
LATR = 4
LONC = 2
OV = 4
MEMBERS = 64
STEPS = 8
PTS = 8
OUT_FEAT = 256
RES_BLOCKS = 16
IN_BLOCKS = 6
N_LAT = 4
N_LON = 8


def draw_intersection(key, part):
    count_all = N_LAT * N_LON * 2
    keys = jax.random.split(jax.random.fold_in(key, 11), count_all)
    orders = jax.vmap(lambda single: jax.random.permutation(single, PTS))(keys)
    orders = orders[:, :OV].reshape(N_LAT, N_LON, 2, OV).astype(jnp.int32)
    counts = jax.random.randint(jax.random.fold_in(key, 23), (N_LAT, N_LON, 2, 1), 1, OV + 1)
    sector = jnp.arange(N_LON, dtype=jnp.int32)[None, :, None, None]
    counts = jnp.where(sector == 0, OV, counts)
    slot = jnp.arange(OV, dtype=jnp.int32)[None, None, None, :]
    lists = jnp.where(slot < counts, orders, -1)
    band = jnp.arange(N_LAT, dtype=jnp.int32)[:, None, None, None]
    side = jnp.arange(2, dtype=jnp.int32)[None, None, :, None]
    polar = (band == 0) & (side == 0) | (band == N_LAT - 1) & (side == 1)
    return jnp.where(polar, -1, lists).astype(jnp.int32)


def levels(stream_key, shape, cuts, smallest, high):
    level = 1.0
    for dim, parts in cuts:
        heights = jax.random.uniform(jax.random.fold_in(jax.random.fold_in(stream_key, 6), dim), (parts,), jnp.float32, smallest / len(cuts), high / len(cuts))
        level = level * jnp.repeat(jnp.exp(heights), shape[dim] // parts).reshape((-1,) + (1,) * (len(shape) - 1 - dim))
    return level


def gaussian(stream_key, extent, width, limit, cuts=(), held_as=jnp.bfloat16):
    loudness = levels(stream_key, extent, cuts, -0.22, 0.18) if cuts else 1.0
    values = jax.random.normal(stream_key, extent, jnp.float32) * width * loudness
    return jnp.minimum(jnp.maximum(values, -limit), limit).astype(held_as)


def setup_inputs(seed: int = 0) -> dict:
    key_of = jax.random.split(jax.random.key(seed), 7)
    initial_state = gaussian(key_of[0], (N_LAT, N_LON, MEMBERS, OUT_FEAT), 1.0, 6.0, ((0, 4), (1, 8)), jnp.float32)
    initial_reservoir = jnp.clip(jax.random.uniform(key_of[1], (N_LAT, N_LON, MEMBERS, N_RES), jnp.float32, -0.8984375, 0.8984375) * levels(key_of[1], (N_LAT, N_LON, MEMBERS, N_RES), ((0, 4), (1, 8)), -0.4, 0.0), -0.8984375, 0.8984375).astype(jnp.bfloat16)
    coupling = gaussian(key_of[2], (N_LAT, N_LON, RES_BLOCKS, NCON, BLOCK, BLOCK), (2 * NCON * BLOCK) ** -0.5, 0.1875, ((0, 4), (1, 8)))
    input_weight = gaussian(key_of[3], (N_LAT, N_LON, RES_BLOCKS, BLOCK, BLOCK), BLOCK ** -0.5, 0.5, ((0, 4), (1, 8)))
    readout = gaussian(key_of[4], (N_LAT, N_LON, N_RES, OUT_FEAT), N_RES ** -0.5, 0.125, ((0, 4), (1, 8)))
    intersection = draw_intersection(jax.random.fold_in(key_of[6], 71), 0)
    return dict(initial_state=initial_state, initial_reservoir=initial_reservoir, coupling=coupling, input_weight=input_weight, readout=readout, intersection=intersection)


def select_points(source, lists):
    bands, sectors, members = source.shape[0], source.shape[1], source.shape[2]
    points = source.astype(jnp.float32).reshape(bands, sectors, members, PTS, VARS)
    onehot = (lists[..., None] == jnp.arange(PTS, dtype=jnp.int32)).astype(jnp.float32)
    picked = jnp.einsum('ijsp,ijmpv->ijmsv', onehot, points)
    return picked.astype(jnp.bfloat16).reshape(bands, sectors, members, OV * VARS)


def band_update(pieces):
    inputs, reservoir, coupling, input_weight, readout = pieces
    sectors, members = reservoir.shape[0], reservoir.shape[1]
    blocks = reservoir.astype(jnp.float32).reshape(sectors, members, RES_BLOCKS, BLOCK)
    linked = np.arange(RES_BLOCKS)[:, None] + np.arange(NCON)[None, :]
    linked = linked % RES_BLOCKS
    gathered = blocks[:, :, linked]
    activation = jnp.einsum('jmbki,jbkio->jmbo', gathered, coupling.astype(jnp.float32))
    chosen = inputs.astype(jnp.float32).reshape(sectors, members, IN_BLOCKS, BLOCK)
    chosen = chosen[:, :, np.arange(RES_BLOCKS) % IN_BLOCKS]
    activation = activation + jnp.einsum('jmbi,jbio->jmbo', chosen, input_weight.astype(jnp.float32))
    fresh = jnp.tanh(activation).astype(jnp.bfloat16).reshape(sectors, members, N_RES)
    widened = fresh.astype(jnp.float32)
    even_nodes = (jnp.arange(N_RES) % 2) == 0
    features = jnp.where(even_nodes, widened * widened, widened).astype(jnp.bfloat16)
    result = jnp.einsum('jmn,jny->jmy', features.astype(jnp.float32), readout.astype(jnp.float32))
    return fresh, result


def reference(initial_state, initial_reservoir, coupling, input_weight, readout, intersection):
    current = initial_state
    reservoir = initial_reservoir
    outputs = []
    for moment in range(STEPS):
        rounded = current.astype(jnp.bfloat16)
        columns = rounded.reshape(N_LAT, N_LON, MEMBERS, LONC, LATR * VARS)
        west_col = jnp.roll(columns[:, :, :, LONC - 1], 1, axis=1)
        east_col = jnp.roll(columns[:, :, :, 0], -1, axis=1)
        empty = jnp.zeros_like(rounded[:1])
        from_north = jnp.concatenate([empty, rounded[:-1]], axis=0)
        from_south = jnp.concatenate([rounded[1:], empty], axis=0)
        north_part = select_points(from_north, intersection[:, :, 0])
        south_part = select_points(from_south, intersection[:, :, 1])
        inputs = jnp.concatenate([rounded, west_col, east_col, north_part, south_part], axis=-1)
        reservoir, current = lax.map(band_update, (inputs, reservoir, coupling, input_weight, readout))
        outputs.append(current)
    return jnp.stack(outputs)
```

```python
import functools

import jax
import jax.numpy as jnp
from jax import lax
from jax.experimental import pallas as pl
from jax.experimental.pallas import tpu as pltpu
from jax.sharding import PartitionSpec as P

VARS = 32
OV = 4
STEPS = 8
BLOCK = 128
MESH = pl.DeviceIdType.MESH


def kernel(
    n_lat,
    n_lon,
    lists,
    state,
    reservoir,
    coupling,
    entry,
    read,
    out,
    u0,
    r,
    cw,
    iw,
    rw,
    nsw,
    acc,
    send,
    we_in,
    ns_in,
    outbuf,
    send_sem,
    recv_sem,
    load_sem,
    out_sem,
):
    members = u0.shape[0]
    blocks = cw.shape[0]
    links = cw.shape[1] // BLOCK
    pairs = blocks // 2
    own_pairs = [m for m in range(pairs) if m % 3 == 0]
    we_pairs = [m for m in range(pairs) if m % 3 == 1]
    ns_pairs = [m for m in range(pairs) if m % 3 == 2]

    band = lax.axis_index("lat")
    sector = lax.axis_index("lon")
    east = (band, lax.rem(sector + 1, n_lon))
    west = (band, lax.rem(sector + n_lon - 1, n_lon))
    south = (lax.rem(band + 1, n_lat), sector)
    north = (lax.rem(band + n_lat - 1, n_lat), sector)
    has_north = band > 0
    has_south = band < n_lat - 1

    loads = [
        pltpu.make_async_copy(src, dst, load_sem.at[i])
        for i, (src, dst) in enumerate(
            [(state, u0), (reservoir, r), (coupling, cw), (entry, iw), (read, rw)]
        )
    ]
    for load in loads:
        load.start()

    barrier = pltpu.get_barrier_semaphore()
    pl.semaphore_signal(barrier, inc=1, device_id=east, device_id_type=MESH)
    pl.semaphore_signal(barrier, inc=1, device_id=west, device_id_type=MESH)

    @pl.when(has_south)
    def _():
        pl.semaphore_signal(barrier, inc=1, device_id=south, device_id_type=MESH)

    @pl.when(has_north)
    def _():
        pl.semaphore_signal(barrier, inc=1, device_id=north, device_id_type=MESH)

    def remote(t, src, dst, side, target):
        return pltpu.make_async_remote_copy(
            src_ref=src,
            dst_ref=dst,
            send_sem=send_sem.at[t, side],
            recv_sem=recv_sem.at[t, side],
            device_id=target,
            device_id_type=MESH,
        )

    def to_east(t):
        return remote(t, send.at[t, 1], we_in.at[t, 0], 0, east)

    def to_west(t):
        return remote(t, send.at[t, 0], we_in.at[t, 1], 1, west)

    def to_south(t):
        return remote(t, send.at[t], ns_in.at[t, 0], 2, south)

    def to_north(t):
        return remote(t, send.at[t], ns_in.at[t, 1], 3, north)

    def start_sends(t):
        to_east(t).start()
        to_west(t).start()

        @pl.when(has_south)
        def _():
            to_south(t).start()

        @pl.when(has_north)
        def _():
            to_north(t).start()

    def wait_sends(t):
        to_east(t).wait_send()
        to_west(t).wait_send()

        @pl.when(has_south)
        def _():
            to_south(t).wait_send()

        @pl.when(has_north)
        def _():
            to_north(t).wait_send()

    def put_state(t, value):
        rounded = value.astype(jnp.bfloat16)
        send[t, 0] = rounded[:, :BLOCK]
        send[t, 1] = rounded[:, BLOCK:]

    def dot(a, b):
        return jnp.dot(a, b, preferred_element_type=jnp.float32)

    loads[0].wait()
    put_state(0, u0[...])
    pl.semaphore_wait(
        barrier, 2 + has_north.astype(jnp.int32) + has_south.astype(jnp.int32)
    )
    start_sends(0)

    @pl.when(jnp.logical_not(has_north))
    def _():
        for t in range(STEPS):
            ns_in[t, 0] = jnp.zeros(ns_in.shape[2:], ns_in.dtype)

    @pl.when(jnp.logical_not(has_south))
    def _():
        for t in range(STEPS):
            ns_in[t, 1] = jnp.zeros(ns_in.shape[2:], ns_in.dtype)

    row = lax.broadcasted_iota(jnp.int32, (2 * BLOCK, BLOCK), 0)
    col = lax.broadcasted_iota(jnp.int32, (2 * BLOCK, BLOCK), 1)
    loads[3].wait()
    for side in range(2):
        target = jnp.full((2 * BLOCK, BLOCK), -VARS, jnp.int32)
        for s in range(OV):
            here = (col >= s * VARS) & (col < (s + 1) * VARS)
            target = jnp.where(here, lists[side, s] * VARS + (col - s * VARS), target)
        onehot = jnp.where(row == target, 1.0, 0.0).astype(jnp.bfloat16)
        for n, m in enumerate(ns_pairs):
            nsw[2 * n + side] = dot(onehot, iw[2 * m + side]).astype(jnp.bfloat16)

    for i in (1, 2, 4):
        loads[i].wait()

    even = lax.broadcasted_iota(jnp.int32, (members, 2 * BLOCK), 1) % 2 == 0

    def couple(b):
        first = min(links, blocks - b)
        total = dot(r[:, b * BLOCK : (b + first) * BLOCK], cw[b, : first * BLOCK])
        if first < links:
            total += dot(r[:, : (links - first) * BLOCK], cw[b, first * BLOCK :])
        return total

    def finish(m, activation):
        held = slice(2 * m * BLOCK, 2 * (m + 1) * BLOCK)
        fresh = jnp.tanh(activation).astype(jnp.bfloat16)
        r[:, held] = fresh
        wide = fresh.astype(jnp.float32)
        features = jnp.where(even, wide * wide, wide).astype(jnp.bfloat16)
        return dot(features, rw[held, :])

    @pl.loop(0, STEPS)
    def _(t):
        own = [send[t, c] for c in range(2)]
        for m in own_pairs + ns_pairs + we_pairs:
            for c in range(2):
                b = 2 * m + c
                total = couple(b)
                if m in own_pairs:
                    total += dot(own[c], iw[b])
                acc[:, b * BLOCK : (b + 1) * BLOCK] = total

        def pair_acc(m):
            return acc[:, 2 * m * BLOCK : 2 * (m + 1) * BLOCK]

        result = sum(finish(m, pair_acc(m)) for m in own_pairs)

        @pl.when(t > 0)
        def _():
            wait_sends(t - 1)
            pltpu.make_async_copy(
                outbuf.at[t - 1], out.at[t - 1], out_sem.at[t - 1]
            ).wait()

        @pl.when(has_north)
        def _():
            to_south(t).wait_recv()

        @pl.when(has_south)
        def _():
            to_north(t).wait_recv()

        sides = [
            jnp.concatenate([ns_in[t, side, 0], ns_in[t, side, 1]], axis=1)
            for side in range(2)
        ]
        for n, m in enumerate(ns_pairs):
            entered = [dot(sides[side], nsw[2 * n + side]) for side in range(2)]
            result += finish(m, pair_acc(m) + jnp.concatenate(entered, axis=1))

        to_east(t).wait_recv()
        to_west(t).wait_recv()
        for m in we_pairs:
            entered = [dot(we_in[t, side], iw[2 * m + side]) for side in range(2)]
            result += finish(m, pair_acc(m) + jnp.concatenate(entered, axis=1))

        @pl.when(t < STEPS - 1)
        def _():
            put_state(t + 1, result)
            start_sends(t + 1)

        outbuf[t] = result
        pltpu.make_async_copy(outbuf.at[t], out.at[t], out_sem.at[t]).start()

    last = STEPS - 1
    wait_sends(last)
    pltpu.make_async_copy(outbuf.at[last], out.at[last], out_sem.at[last]).wait()


def per_device(n_lat, n_lon, initial_state, initial_reservoir, coupling, input_weight, readout, intersection):
    state = initial_state[0, 0]
    reservoir = initial_reservoir[0, 0]
    entry = input_weight[0, 0]
    read = readout[0, 0]
    lists = intersection[0, 0]
    members, features = state.shape
    nodes = reservoir.shape[1]
    blocks, links = coupling.shape[2], coupling.shape[3]
    weights = coupling[0, 0].reshape(blocks, links * BLOCK, BLOCK)
    ns_count = 2 * len([m for m in range(blocks // 2) if m % 3 == 2])
    hbm = pl.BlockSpec(memory_space=pltpu.MemorySpace.HBM)
    bf16, f32 = jnp.bfloat16, jnp.float32
    forecast = pl.pallas_call(
        functools.partial(kernel, n_lat, n_lon),
        out_shape=jax.ShapeDtypeStruct((STEPS, members, features), f32),
        in_specs=[pl.BlockSpec(memory_space=pltpu.MemorySpace.SMEM)] + [hbm] * 5,
        out_specs=hbm,
        scratch_shapes=[
            pltpu.VMEM((members, features), f32),
            pltpu.VMEM((members, nodes), bf16),
            pltpu.VMEM((blocks, links * BLOCK, BLOCK), bf16),
            pltpu.VMEM((blocks, BLOCK, BLOCK), bf16),
            pltpu.VMEM((nodes, features), bf16),
            pltpu.VMEM((ns_count, 2 * BLOCK, BLOCK), bf16),
            pltpu.VMEM((members, nodes), f32),
            pltpu.VMEM((STEPS, 2, members, BLOCK), bf16),
            pltpu.VMEM((STEPS, 2, members, BLOCK), bf16),
            pltpu.VMEM((STEPS, 2, 2, members, BLOCK), bf16),
            pltpu.VMEM((STEPS, members, features), f32),
            pltpu.SemaphoreType.DMA((STEPS, 4)),
            pltpu.SemaphoreType.DMA((STEPS, 4)),
            pltpu.SemaphoreType.DMA((5,)),
            pltpu.SemaphoreType.DMA((STEPS,)),
        ],
        compiler_params=pltpu.CompilerParams(
            collective_id=0, has_side_effects=True, vmem_limit_bytes=24 * 1024 * 1024
        ),
    )(lists, state, reservoir, weights, entry, read)
    return forecast[:, None, None]


def solution(mesh):
    in_specs = (
        P("lat", "lon", None, None),
        P("lat", "lon", None, None),
        P("lat", "lon", None, None, None, None),
        P("lat", "lon", None, None, None),
        P("lat", "lon", None, None),
        P("lat", "lon", None, None),
    )
    out_specs = P(None, "lat", "lon", None, None)
    run = functools.partial(per_device, mesh.shape["lat"], mesh.shape["lon"])
    return jax.shard_map(
        run, mesh=mesh, in_specs=in_specs, out_specs=out_specs, check_vma=False
    )
```

```python
import functools

import jax
import jax.numpy as jnp
from jax import lax
from jax.experimental import pallas as pl
from jax.experimental.pallas import tpu as pltpu
from jax.sharding import PartitionSpec as P

VARS = 32
OV = 4
STEPS = 8
BLOCK = 128
MESH = pl.DeviceIdType.MESH


def kernel(
    n_lat,
    n_lon,
    lists,
    state,
    reservoir,
    coupling,
    entry,
    read,
    out,
    u0,
    r0,
    r,
    cw,
    iw,
    rw,
    nsw,
    acc,
    send,
    we_in,
    ns_in,
    outbuf,
    send_sem,
    recv_sem,
    load_sem,
    out_sem,
):
    members = u0.shape[0]
    blocks = cw.shape[0]
    links = cw.shape[1] // BLOCK
    pairs = blocks // 2
    own_pairs = [m for m in range(pairs) if m % 3 == 0]
    we_pairs = [m for m in range(pairs) if m % 3 == 1]
    ns_pairs = [m for m in range(pairs) if m % 3 == 2]
    own_blocks = [2 * m + c for m in own_pairs for c in range(2)]
    ns_blocks = [2 * m + c for m in ns_pairs for c in range(2)]

    band = lax.axis_index("lat")
    sector = lax.axis_index("lon")
    east = (band, lax.rem(sector + 1, n_lon))
    west = (band, lax.rem(sector + n_lon - 1, n_lon))
    far = lax.rem(sector, 2)
    near = 1 - far
    south = (lax.rem(band + 1, n_lat), sector)
    north = (lax.rem(band + n_lat - 1, n_lat), sector)
    has_north = band > 0
    has_south = band < n_lat - 1

    loads = [
        pltpu.make_async_copy(src, dst, load_sem.at[i])
        for i, (src, dst) in enumerate(
            [(state, u0), (entry, iw), (reservoir, r0), (coupling, cw), (read, rw)]
        )
    ]
    for load in loads:
        load.start()

    barrier = pltpu.get_barrier_semaphore()
    pl.semaphore_signal(barrier, inc=1, device_id=east, device_id_type=MESH)
    pl.semaphore_signal(barrier, inc=1, device_id=west, device_id_type=MESH)

    @pl.when(has_south)
    def _():
        pl.semaphore_signal(barrier, inc=1, device_id=south, device_id_type=MESH)

    @pl.when(has_north)
    def _():
        pl.semaphore_signal(barrier, inc=1, device_id=north, device_id_type=MESH)

    def remote(t, src, dst, side, target):
        return pltpu.make_async_remote_copy(
            src_ref=src,
            dst_ref=dst,
            send_sem=send_sem.at[t, side],
            recv_sem=recv_sem.at[t, side],
            device_id=target,
            device_id_type=MESH,
        )

    def to_lon(t, side):
        target = (band, lax.rem(sector + 2 * side - 1 + n_lon, n_lon))
        return remote(t, send.at[t, side], we_in.at[t, 1 - side], 1 - side, target)

    def to_south(t):
        return remote(t, send.at[t], ns_in.at[t, 0], 2, south)

    def to_north(t):
        return remote(t, send.at[t], ns_in.at[t, 1], 3, north)

    def start_sends(t):
        to_lon(t, far).start()
        to_lon(t, near).start()

        @pl.when(has_south)
        def _():
            to_south(t).start()

        @pl.when(has_north)
        def _():
            to_north(t).start()

    def wait_sends(t):
        to_lon(t, far).wait_send()
        to_lon(t, near).wait_send()

        @pl.when(has_south)
        def _():
            to_south(t).wait_send()

        @pl.when(has_north)
        def _():
            to_north(t).wait_send()

    def put_state(t, value):
        rounded = value.astype(jnp.bfloat16)
        send[t, 0] = rounded[:, :BLOCK]
        send[t, 1] = rounded[:, BLOCK:]

    def dot(a, b):
        return jnp.dot(a, b, preferred_element_type=jnp.float32)

    loads[0].wait()
    put_state(0, u0[...])
    pl.semaphore_wait(
        barrier, 2 + has_north.astype(jnp.int32) + has_south.astype(jnp.int32)
    )
    start_sends(0)

    @pl.when(jnp.logical_not(has_north))
    def _():
        for t in range(STEPS):
            ns_in[t, 0] = jnp.zeros(ns_in.shape[2:], ns_in.dtype)

    @pl.when(jnp.logical_not(has_south))
    def _():
        for t in range(STEPS):
            ns_in[t, 1] = jnp.zeros(ns_in.shape[2:], ns_in.dtype)

    row = lax.broadcasted_iota(jnp.int32, (2 * BLOCK, BLOCK), 0)
    col = lax.broadcasted_iota(jnp.int32, (2 * BLOCK, BLOCK), 1)
    loads[1].wait()
    for side in range(2):
        target = jnp.full((2 * BLOCK, BLOCK), -VARS, jnp.int32)
        for s in range(OV):
            here = (col >= s * VARS) & (col < (s + 1) * VARS)
            target = jnp.where(here, lists[side, s] * VARS + (col - s * VARS), target)
        onehot = jnp.where(row == target, 1.0, 0.0).astype(jnp.bfloat16)
        for n, m in enumerate(ns_pairs):
            nsw[2 * n + side] = dot(onehot, iw[2 * m + side]).astype(jnp.bfloat16)

    loads[2].wait()
    for b in range(blocks):
        r[b] = r0[:, b * BLOCK : (b + 1) * BLOCK]
    loads[3].wait()
    loads[4].wait()

    even = lax.broadcasted_iota(jnp.int32, (members, BLOCK), 1) % 2 == 0

    def couple(b):
        linked = [r[(b + k) % blocks] for k in range(links)]
        return dot(jnp.concatenate(linked, axis=1), cw[b])

    def finish(indices, activations):
        features = []
        for b, activation in zip(indices, activations):
            fresh = jnp.tanh(activation).astype(jnp.bfloat16)
            r[b] = fresh
            wide = fresh.astype(jnp.float32)
            features.append(jnp.where(even, wide * wide, wide).astype(jnp.bfloat16))
        return dot(
            jnp.concatenate(features, axis=1),
            jnp.concatenate([rw[b] for b in indices], axis=0),
        )

    @pl.loop(0, STEPS)
    def _(t):
        own = [send[t, c] for c in range(2)]
        for b in range(blocks):
            total = couple(b)
            if b in own_blocks:
                total += dot(own[b % 2], iw[b])
            acc[b] = total

        result = finish(own_blocks, [acc[b] for b in own_blocks])

        @pl.when(t > 0)
        def _():
            wait_sends(t - 1)
            pltpu.make_async_copy(
                outbuf.at[t - 1], out.at[t - 1], out_sem.at[t - 1]
            ).wait()

        @pl.when(has_north)
        def _():
            to_south(t).wait_recv()

        @pl.when(has_south)
        def _():
            to_north(t).wait_recv()

        sides = [
            jnp.concatenate([ns_in[t, side, 0], ns_in[t, side, 1]], axis=1)
            for side in range(2)
        ]
        result += finish(
            ns_blocks,
            [acc[b] + dot(sides[b % 2], nsw[n]) for n, b in enumerate(ns_blocks)],
        )

        for side in (near, far):
            to_lon(t, 1 - side).wait_recv()
            indices = [2 * m + side for m in we_pairs]
            entered = dot(
                we_in[t, side], jnp.concatenate([iw[b] for b in indices], axis=1)
            )
            result += finish(
                indices,
                [
                    acc[b] + entered[:, n * BLOCK : (n + 1) * BLOCK]
                    for n, b in enumerate(indices)
                ],
            )

        @pl.when(t < STEPS - 1)
        def _():
            put_state(t + 1, result)
            start_sends(t + 1)

        outbuf[t] = result
        pltpu.make_async_copy(outbuf.at[t], out.at[t], out_sem.at[t]).start()

    last = STEPS - 1
    wait_sends(last)
    pltpu.make_async_copy(outbuf.at[last], out.at[last], out_sem.at[last]).wait()


def per_device(n_lat, n_lon, initial_state, initial_reservoir, coupling, input_weight, readout, intersection):
    state = initial_state[0, 0]
    reservoir = initial_reservoir[0, 0]
    entry = input_weight[0, 0]
    lists = intersection[0, 0]
    members, features = state.shape
    nodes = reservoir.shape[1]
    blocks, links = coupling.shape[2], coupling.shape[3]
    read = readout[0, 0].reshape(blocks, BLOCK, features)
    weights = coupling[0, 0].reshape(blocks, links * BLOCK, BLOCK)
    ns_count = 2 * len([m for m in range(blocks // 2) if m % 3 == 2])
    hbm = pl.BlockSpec(memory_space=pltpu.MemorySpace.HBM)
    bf16, f32 = jnp.bfloat16, jnp.float32
    forecast = pl.pallas_call(
        functools.partial(kernel, n_lat, n_lon),
        out_shape=jax.ShapeDtypeStruct((STEPS, members, features), f32),
        in_specs=[pl.BlockSpec(memory_space=pltpu.MemorySpace.SMEM)] + [hbm] * 5,
        out_specs=hbm,
        scratch_shapes=[
            pltpu.VMEM((members, features), f32),
            pltpu.VMEM((members, nodes), bf16),
            pltpu.VMEM((blocks, members, BLOCK), bf16),
            pltpu.VMEM((blocks, links * BLOCK, BLOCK), bf16),
            pltpu.VMEM((blocks, BLOCK, BLOCK), bf16),
            pltpu.VMEM((blocks, BLOCK, features), bf16),
            pltpu.VMEM((ns_count, 2 * BLOCK, BLOCK), bf16),
            pltpu.VMEM((blocks, members, BLOCK), f32),
            pltpu.VMEM((STEPS, 2, members, BLOCK), bf16),
            pltpu.VMEM((STEPS, 2, members, BLOCK), bf16),
            pltpu.VMEM((STEPS, 2, 2, members, BLOCK), bf16),
            pltpu.VMEM((STEPS, members, features), f32),
            pltpu.SemaphoreType.DMA((STEPS, 4)),
            pltpu.SemaphoreType.DMA((STEPS, 4)),
            pltpu.SemaphoreType.DMA((5,)),
            pltpu.SemaphoreType.DMA((STEPS,)),
        ],
        compiler_params=pltpu.CompilerParams(
            collective_id=0, has_side_effects=True, vmem_limit_bytes=63 * 1024 * 1024
        ),
    )(lists, state, reservoir, weights, entry, read)
    return forecast[:, None, None]


def solution(mesh):
    in_specs = (
        P("lat", "lon", None, None),
        P("lat", "lon", None, None),
        P("lat", "lon", None, None, None, None),
        P("lat", "lon", None, None, None),
        P("lat", "lon", None, None),
        P("lat", "lon", None, None),
    )
    out_specs = P(None, "lat", "lon", None, None)
    run = functools.partial(per_device, mesh.shape["lat"], mesh.shape["lon"])
    return jax.shard_map(
        run, mesh=mesh, in_specs=in_specs, out_specs=out_specs, check_vma=False
    )
```

```python
import functools

import jax
import jax.numpy as jnp
from jax import lax
from jax.experimental import pallas as pl
from jax.experimental.pallas import tpu as pltpu
from jax.sharding import PartitionSpec as P

VARS = 32
OV = 4
STEPS = 8
BLOCK = 128
MESH = pl.DeviceIdType.MESH


def kernel(
    n_lat,
    n_lon,
    lists,
    state,
    reservoir,
    coupling,
    entry,
    read,
    out,
    u0,
    r0,
    r,
    cw,
    iw,
    rw,
    nsw,
    acc,
    send,
    we_in,
    ns_in,
    outbuf,
    send_sem,
    recv_sem,
    load_sem,
    pair_sem,
    out_sem,
):
    members = u0.shape[0]
    blocks = coupling.shape[0]
    depth = coupling.shape[1]
    links = depth // BLOCK
    pairs = blocks // 2
    own_pairs = [m for m in range(pairs) if m % 3 == 0]
    we_pairs = [m for m in range(pairs) if m % 3 == 1]
    ns_pairs = [m for m in range(pairs) if m % 3 == 2]
    own_blocks = [2 * m + c for m in own_pairs for c in range(2)]
    ns_blocks = [2 * m + c for m in ns_pairs for c in range(2)]

    band = lax.axis_index("lat")
    sector = lax.axis_index("lon")
    east = (band, lax.rem(sector + 1, n_lon))
    west = (band, lax.rem(sector + n_lon - 1, n_lon))
    far = lax.rem(sector, 2)
    near = 1 - far
    south = (lax.rem(band + 1, n_lat), sector)
    north = (lax.rem(band + n_lat - 1, n_lat), sector)
    has_north = band > 0
    has_south = band < n_lat - 1

    barrier = pltpu.get_barrier_semaphore()
    pl.semaphore_signal(barrier, inc=1, device_id=east, device_id_type=MESH)
    pl.semaphore_signal(barrier, inc=1, device_id=west, device_id_type=MESH)

    @pl.when(has_south)
    def _():
        pl.semaphore_signal(barrier, inc=1, device_id=south, device_id_type=MESH)

    @pl.when(has_north)
    def _():
        pl.semaphore_signal(barrier, inc=1, device_id=north, device_id_type=MESH)

    loads = [
        pltpu.make_async_copy(src, dst, load_sem.at[i])
        for i, (src, dst) in enumerate(
            [(state, u0), (entry, iw), (reservoir, r0), (read, rw)]
        )
    ]
    ends = (depth + BLOCK, depth + 2 * BLOCK, depth + 3 * BLOCK)
    places = []
    for m in range(pairs):
        for c in range(2):
            lanes = pl.ds(c * BLOCK, BLOCK)
            places.append((coupling.at[2 * m + c], cw.at[m, pl.ds(c * BLOCK, depth), lanes]))
            if m in own_pairs:
                rows = pl.ds(ends[c], BLOCK)
                places.append((entry.at[2 * m + c], cw.at[m, rows, lanes]))
    pieces = [
        pltpu.make_async_copy(src, dst, pair_sem.at[i])
        for i, (src, dst) in enumerate(places)
    ]
    for load in loads + pieces:
        load.start()

    blank = jnp.zeros((BLOCK, BLOCK), cw.dtype)
    for m in range(pairs):
        cw[m, :BLOCK, BLOCK:] = blank
        cw[m, depth : ends[0], :BLOCK] = blank
        if m in own_pairs:
            cw[m, ends[1] : ends[2], :BLOCK] = blank
            cw[m, ends[0] : ends[1], BLOCK:] = blank

    def remote(t, src, dst, side, target):
        return pltpu.make_async_remote_copy(
            src_ref=src,
            dst_ref=dst,
            send_sem=send_sem.at[t, side],
            recv_sem=recv_sem.at[t, side],
            device_id=target,
            device_id_type=MESH,
        )

    def to_lon(t, side):
        target = (band, lax.rem(sector + 2 * side - 1 + n_lon, n_lon))
        return remote(t, send.at[t, side], we_in.at[t, 1 - side], 1 - side, target)

    def to_south(t):
        return remote(t, send.at[t], ns_in.at[t, 0], 2, south)

    def to_north(t):
        return remote(t, send.at[t], ns_in.at[t, 1], 3, north)

    def start_sends(t):
        to_lon(t, far).start()
        to_lon(t, near).start()

        @pl.when(has_south)
        def _():
            to_south(t).start()

        @pl.when(has_north)
        def _():
            to_north(t).start()

    def wait_sends(t):
        to_lon(t, far).wait_send()
        to_lon(t, near).wait_send()

        @pl.when(has_south)
        def _():
            to_south(t).wait_send()

        @pl.when(has_north)
        def _():
            to_north(t).wait_send()

    def put_state(t, value):
        rounded = value.astype(jnp.bfloat16)
        send[t, 0] = rounded[:, :BLOCK]
        send[t, 1] = rounded[:, BLOCK:]

    def dot(a, b):
        return jnp.dot(a, b, preferred_element_type=jnp.float32)

    loads[0].wait()
    put_state(0, u0[...])
    pl.semaphore_wait(
        barrier, 2 + has_north.astype(jnp.int32) + has_south.astype(jnp.int32)
    )
    start_sends(0)

    @pl.when(jnp.logical_not(has_north))
    def _():
        for t in range(STEPS):
            ns_in[t, 0] = jnp.zeros(ns_in.shape[2:], ns_in.dtype)

    @pl.when(jnp.logical_not(has_south))
    def _():
        for t in range(STEPS):
            ns_in[t, 1] = jnp.zeros(ns_in.shape[2:], ns_in.dtype)

    row = lax.broadcasted_iota(jnp.int32, (2 * BLOCK, BLOCK), 0)
    col = lax.broadcasted_iota(jnp.int32, (2 * BLOCK, BLOCK), 1)
    loads[1].wait()
    for side in range(2):
        target = jnp.full((2 * BLOCK, BLOCK), -VARS, jnp.int32)
        for s in range(OV):
            here = (col >= s * VARS) & (col < (s + 1) * VARS)
            target = jnp.where(here, lists[side, s] * VARS + (col - s * VARS), target)
        onehot = jnp.where(row == target, 1.0, 0.0).astype(jnp.bfloat16)
        for n, m in enumerate(ns_pairs):
            nsw[2 * n + side] = dot(onehot, iw[2 * m + side]).astype(jnp.bfloat16)

    loads[2].wait()
    for b in range(blocks):
        r[b] = r0[:, b * BLOCK : (b + 1) * BLOCK]
    for load in loads[3:] + pieces:
        load.wait()

    even = lax.broadcasted_iota(jnp.int32, (members, BLOCK), 1) % 2 == 0

    def couple(m, extra):
        linked = [r[(2 * m + k) % blocks] for k in range(links + 1)] + extra
        return dot(jnp.concatenate(linked, axis=1), cw[m, : len(linked) * BLOCK])

    def finish(indices, activations):
        features = []
        for b, activation in zip(indices, activations):
            fresh = jnp.tanh(activation).astype(jnp.bfloat16)
            r[b] = fresh
            wide = fresh.astype(jnp.float32)
            features.append(jnp.where(even, wide * wide, wide).astype(jnp.bfloat16))
        return dot(
            jnp.concatenate(features, axis=1),
            jnp.concatenate([rw[b] for b in indices], axis=0),
        )

    @pl.loop(0, STEPS)
    def _(t):
        own = [send[t, c] for c in range(2)]
        for m in range(pairs):
            total = couple(m, own if m in own_pairs else [])
            acc[2 * m] = total[:, :BLOCK]
            acc[2 * m + 1] = total[:, BLOCK:]

        result = finish(own_blocks, [acc[b] for b in own_blocks])

        @pl.when(t > 0)
        def _():
            wait_sends(t - 1)
            pltpu.make_async_copy(
                outbuf.at[t - 1], out.at[t - 1], out_sem.at[t - 1]
            ).wait()

        @pl.when(has_north)
        def _():
            to_south(t).wait_recv()

        @pl.when(has_south)
        def _():
            to_north(t).wait_recv()

        sides = [
            jnp.concatenate([ns_in[t, side, 0], ns_in[t, side, 1]], axis=1)
            for side in range(2)
        ]
        result += finish(
            ns_blocks,
            [acc[b] + dot(sides[b % 2], nsw[n]) for n, b in enumerate(ns_blocks)],
        )

        for side in (near, far):
            to_lon(t, 1 - side).wait_recv()
            indices = [2 * m + side for m in we_pairs]
            entered = dot(
                we_in[t, side], jnp.concatenate([iw[b] for b in indices], axis=1)
            )
            result += finish(
                indices,
                [
                    acc[b] + entered[:, n * BLOCK : (n + 1) * BLOCK]
                    for n, b in enumerate(indices)
                ],
            )

        @pl.when(t < STEPS - 1)
        def _():
            put_state(t + 1, result)
            start_sends(t + 1)

        outbuf[t] = result
        pltpu.make_async_copy(outbuf.at[t], out.at[t], out_sem.at[t]).start()

    last = STEPS - 1
    wait_sends(last)
    pltpu.make_async_copy(outbuf.at[last], out.at[last], out_sem.at[last]).wait()


def per_device(n_lat, n_lon, initial_state, initial_reservoir, coupling, input_weight, readout, intersection):
    state = initial_state[0, 0]
    reservoir = initial_reservoir[0, 0]
    entry = input_weight[0, 0]
    lists = intersection[0, 0]
    members, features = state.shape
    nodes = reservoir.shape[1]
    blocks, links = coupling.shape[2], coupling.shape[3]
    read = readout[0, 0].reshape(blocks, BLOCK, features)
    weights = coupling[0, 0].reshape(blocks, links * BLOCK, BLOCK)
    ns_count = 2 * len([m for m in range(blocks // 2) if m % 3 == 2])
    hbm = pl.BlockSpec(memory_space=pltpu.MemorySpace.HBM)
    bf16, f32 = jnp.bfloat16, jnp.float32
    forecast = pl.pallas_call(
        functools.partial(kernel, n_lat, n_lon),
        out_shape=jax.ShapeDtypeStruct((STEPS, members, features), f32),
        in_specs=[pl.BlockSpec(memory_space=pltpu.MemorySpace.SMEM)] + [hbm] * 5,
        out_specs=hbm,
        scratch_shapes=[
            pltpu.VMEM((members, features), f32),
            pltpu.VMEM((members, nodes), bf16),
            pltpu.VMEM((blocks, members, BLOCK), bf16),
            pltpu.VMEM((blocks // 2, (links + 3) * BLOCK, 2 * BLOCK), bf16),
            pltpu.VMEM((blocks, BLOCK, BLOCK), bf16),
            pltpu.VMEM((blocks, BLOCK, features), bf16),
            pltpu.VMEM((ns_count, 2 * BLOCK, BLOCK), bf16),
            pltpu.VMEM((blocks, members, BLOCK), f32),
            pltpu.VMEM((STEPS, 2, members, BLOCK), bf16),
            pltpu.VMEM((STEPS, 2, members, BLOCK), bf16),
            pltpu.VMEM((STEPS, 2, 2, members, BLOCK), bf16),
            pltpu.VMEM((STEPS, members, features), f32),
            pltpu.SemaphoreType.DMA((STEPS, 4)),
            pltpu.SemaphoreType.DMA((STEPS, 4)),
            pltpu.SemaphoreType.DMA((4,)),
            pltpu.SemaphoreType.DMA((2 * blocks,)),
            pltpu.SemaphoreType.DMA((STEPS,)),
        ],
        compiler_params=pltpu.CompilerParams(
            collective_id=0, has_side_effects=True, vmem_limit_bytes=63 * 1024 * 1024
        ),
    )(lists, state, reservoir, weights, entry, read)
    return forecast[:, None, None]


def solution(mesh):
    in_specs = (
        P("lat", "lon", None, None),
        P("lat", "lon", None, None),
        P("lat", "lon", None, None, None, None),
        P("lat", "lon", None, None, None),
        P("lat", "lon", None, None),
        P("lat", "lon", None, None),
    )
    out_specs = P(None, "lat", "lon", None, None)
    run = functools.partial(per_device, mesh.shape["lat"], mesh.shape["lon"])
    return jax.shard_map(
        run, mesh=mesh, in_specs=in_specs, out_specs=out_specs, check_vma=False
    )
```

```python
import functools

import jax
import jax.numpy as jnp
from jax import lax
from jax.experimental import pallas as pl
from jax.experimental.pallas import tpu as pltpu
from jax.sharding import PartitionSpec as P

VARS = 32
OV = 4
STEPS = 8
PARTS = 2
BLOCK = 128
MESH = pl.DeviceIdType.MESH


def kernel(
    n_lat,
    n_lon,
    lists,
    state,
    reservoir,
    coupling,
    entry,
    read,
    out,
    u0,
    r0,
    r,
    cw,
    iw,
    rw,
    nsw,
    acc,
    send,
    we_in,
    ns_in,
    outbuf,
    send_sem,
    recv_sem,
    load_sem,
    out_sem,
):
    members = u0.shape[0]
    blocks = cw.shape[0]
    links = cw.shape[1] // BLOCK
    pairs = blocks // 2
    own_pairs = [m for m in range(pairs) if m % 3 == 0]
    we_pairs = [m for m in range(pairs) if m % 3 == 1]
    ns_pairs = [m for m in range(pairs) if m % 3 == 2]
    own_blocks = [2 * m + c for m in own_pairs for c in range(2)]
    ns_blocks = [2 * m + c for m in ns_pairs for c in range(2)]

    band = lax.axis_index("lat")
    sector = lax.axis_index("lon")
    east = (band, lax.rem(sector + 1, n_lon))
    west = (band, lax.rem(sector + n_lon - 1, n_lon))
    size = members // PARTS
    far = lax.rem(sector, 2)
    near = 1 - far
    south = (lax.rem(band + 1, n_lat), sector)
    north = (lax.rem(band + n_lat - 1, n_lat), sector)
    has_north = band > 0
    has_south = band < n_lat - 1

    barrier = pltpu.get_barrier_semaphore()
    pl.semaphore_signal(barrier, inc=1, device_id=east, device_id_type=MESH)
    pl.semaphore_signal(barrier, inc=1, device_id=west, device_id_type=MESH)

    @pl.when(has_south)
    def _():
        pl.semaphore_signal(barrier, inc=1, device_id=south, device_id_type=MESH)

    @pl.when(has_north)
    def _():
        pl.semaphore_signal(barrier, inc=1, device_id=north, device_id_type=MESH)

    loads = [
        pltpu.make_async_copy(src, dst, load_sem.at[i])
        for i, (src, dst) in enumerate(
            [(state, u0), (entry, iw), (reservoir, r0), (coupling, cw), (read, rw)]
        )
    ]
    for load in loads:
        load.start()

    def remote(t, src, dst, slot, target):
        return pltpu.make_async_remote_copy(
            src_ref=src,
            dst_ref=dst,
            send_sem=send_sem.at[t, slot],
            recv_sem=recv_sem.at[t, slot],
            device_id=target,
            device_id_type=MESH,
        )

    def to_lon(t, side, part):
        target = (band, lax.rem(sector + 2 * side - 1 + n_lon, n_lon))
        rows = pl.ds(part * size, size)
        return remote(
            t,
            send.at[t, side, rows],
            we_in.at[t, 1 - side, rows],
            2 + (1 - side) * PARTS + part,
            target,
        )

    def to_south(t):
        return remote(t, send.at[t], ns_in.at[t, 0], 0, south)

    def to_north(t):
        return remote(t, send.at[t], ns_in.at[t, 1], 1, north)

    def start_sends(t):
        for part in range(PARTS):
            to_lon(t, near, part).start()

        @pl.when(has_south)
        def _():
            to_south(t).start()

        @pl.when(has_north)
        def _():
            to_north(t).start()

    def wait_sends(t):
        for part in range(PARTS):
            to_lon(t, far, part).wait_send()
            to_lon(t, near, part).wait_send()

        @pl.when(has_south)
        def _():
            to_south(t).wait_send()

        @pl.when(has_north)
        def _():
            to_north(t).wait_send()

    def put_state(t, part, value):
        rounded = value.astype(jnp.bfloat16)
        rows = slice(part * size, (part + 1) * size)
        send[t, 0, rows] = rounded[:, :BLOCK]
        send[t, 1, rows] = rounded[:, BLOCK:]

    def dot(a, b):
        return jnp.dot(a, b, preferred_element_type=jnp.float32)

    loads[0].wait()
    for part in range(PARTS):
        put_state(0, part, u0[part * size : (part + 1) * size, :])
    pl.semaphore_wait(
        barrier, 2 + has_north.astype(jnp.int32) + has_south.astype(jnp.int32)
    )
    for part in range(PARTS):
        to_lon(0, far, part).start()
    start_sends(0)

    @pl.when(jnp.logical_not(has_north))
    def _():
        for t in range(STEPS):
            ns_in[t, 0] = jnp.zeros(ns_in.shape[2:], ns_in.dtype)

    @pl.when(jnp.logical_not(has_south))
    def _():
        for t in range(STEPS):
            ns_in[t, 1] = jnp.zeros(ns_in.shape[2:], ns_in.dtype)

    row = lax.broadcasted_iota(jnp.int32, (2 * BLOCK, BLOCK), 0)
    col = lax.broadcasted_iota(jnp.int32, (2 * BLOCK, BLOCK), 1)
    loads[1].wait()
    for side in range(2):
        target = jnp.full((2 * BLOCK, BLOCK), -VARS, jnp.int32)
        for s in range(OV):
            here = (col >= s * VARS) & (col < (s + 1) * VARS)
            target = jnp.where(here, lists[side, s] * VARS + (col - s * VARS), target)
        onehot = jnp.where(row == target, 1.0, 0.0).astype(jnp.bfloat16)
        for n, m in enumerate(ns_pairs):
            nsw[2 * n + side] = dot(onehot, iw[2 * m + side]).astype(jnp.bfloat16)

    loads[2].wait()
    for b in range(blocks):
        r[b] = r0[:, b * BLOCK : (b + 1) * BLOCK]
    loads[3].wait()
    loads[4].wait()

    def couple(b):
        linked = [r[(b + k) % blocks] for k in range(links)]
        return dot(jnp.concatenate(linked, axis=1), cw[b])

    def finish(indices, activations, rows=slice(None)):
        even = lax.broadcasted_iota(jnp.int32, activations[0].shape, 1) % 2 == 0
        features = []
        for b, activation in zip(indices, activations):
            fresh = jnp.tanh(activation).astype(jnp.bfloat16)
            r[b, rows] = fresh
            wide = fresh.astype(jnp.float32)
            features.append(jnp.where(even, wide * wide, wide).astype(jnp.bfloat16))
        return dot(
            jnp.concatenate(features, axis=1),
            jnp.concatenate([rw[b] for b in indices], axis=0),
        )

    @pl.loop(0, STEPS)
    def _(t):
        own = [send[t, c] for c in range(2)]
        for b in range(blocks):
            total = couple(b)
            if b in own_blocks:
                total += dot(own[b % 2], iw[b])
            acc[b] = total

        result = finish(own_blocks, [acc[b] for b in own_blocks])

        @pl.when(t > 0)
        def _():
            wait_sends(t - 1)
            pltpu.make_async_copy(
                outbuf.at[t - 1], out.at[t - 1], out_sem.at[t - 1]
            ).wait()

        @pl.when(has_north)
        def _():
            to_south(t).wait_recv()

        @pl.when(has_south)
        def _():
            to_north(t).wait_recv()

        sides = [
            jnp.concatenate([ns_in[t, side, 0], ns_in[t, side, 1]], axis=1)
            for side in range(2)
        ]
        result += finish(
            ns_blocks,
            [acc[b] + dot(sides[b % 2], nsw[n]) for n, b in enumerate(ns_blocks)],
        )

        def finish_side(side, rows):
            indices = [2 * m + side for m in we_pairs]
            entered = dot(
                we_in[t, side, rows], jnp.concatenate([iw[b] for b in indices], axis=1)
            )
            activations = [
                acc[b, rows] + entered[:, n * BLOCK : (n + 1) * BLOCK]
                for n, b in enumerate(indices)
            ]
            return finish(indices, activations, rows)

        for part in range(PARTS):
            to_lon(t, 1 - near, part).wait_recv()
        result += finish_side(near, slice(0, members))

        for part in range(PARTS):
            rows = slice(part * size, (part + 1) * size)
            to_lon(t, 1 - far, part).wait_recv()
            value = result[rows] + finish_side(far, rows)

            @pl.when(t < STEPS - 1)
            def _():
                put_state(t + 1, part, value)
                to_lon(t + 1, far, part).start()

            outbuf[t, rows] = value

        @pl.when(t < STEPS - 1)
        def _():
            start_sends(t + 1)

        pltpu.make_async_copy(outbuf.at[t], out.at[t], out_sem.at[t]).start()

    last = STEPS - 1
    wait_sends(last)
    pltpu.make_async_copy(outbuf.at[last], out.at[last], out_sem.at[last]).wait()


def per_device(n_lat, n_lon, initial_state, initial_reservoir, coupling, input_weight, readout, intersection):
    state = initial_state[0, 0]
    reservoir = initial_reservoir[0, 0]
    entry = input_weight[0, 0]
    lists = intersection[0, 0]
    members, features = state.shape
    nodes = reservoir.shape[1]
    blocks, links = coupling.shape[2], coupling.shape[3]
    read = readout[0, 0].reshape(blocks, BLOCK, features)
    weights = coupling[0, 0].reshape(blocks, links * BLOCK, BLOCK)
    ns_count = 2 * len([m for m in range(blocks // 2) if m % 3 == 2])
    hbm = pl.BlockSpec(memory_space=pltpu.MemorySpace.HBM)
    bf16, f32 = jnp.bfloat16, jnp.float32
    forecast = pl.pallas_call(
        functools.partial(kernel, n_lat, n_lon),
        out_shape=jax.ShapeDtypeStruct((STEPS, members, features), f32),
        in_specs=[pl.BlockSpec(memory_space=pltpu.MemorySpace.SMEM)] + [hbm] * 5,
        out_specs=hbm,
        scratch_shapes=[
            pltpu.VMEM((members, features), f32),
            pltpu.VMEM((members, nodes), bf16),
            pltpu.VMEM((blocks, members, BLOCK), bf16),
            pltpu.VMEM((blocks, links * BLOCK, BLOCK), bf16),
            pltpu.VMEM((blocks, BLOCK, BLOCK), bf16),
            pltpu.VMEM((blocks, BLOCK, features), bf16),
            pltpu.VMEM((ns_count, 2 * BLOCK, BLOCK), bf16),
            pltpu.VMEM((blocks, members, BLOCK), f32),
            pltpu.VMEM((STEPS, 2, members, BLOCK), bf16),
            pltpu.VMEM((STEPS, 2, members, BLOCK), bf16),
            pltpu.VMEM((STEPS, 2, 2, members, BLOCK), bf16),
            pltpu.VMEM((STEPS, members, features), f32),
            pltpu.SemaphoreType.DMA((STEPS, 2 + 2 * PARTS)),
            pltpu.SemaphoreType.DMA((STEPS, 2 + 2 * PARTS)),
            pltpu.SemaphoreType.DMA((5,)),
            pltpu.SemaphoreType.DMA((STEPS,)),
        ],
        compiler_params=pltpu.CompilerParams(
            collective_id=0, has_side_effects=True, vmem_limit_bytes=63 * 1024 * 1024
        ),
    )(lists, state, reservoir, weights, entry, read)
    return forecast[:, None, None]


def solution(mesh):
    in_specs = (
        P("lat", "lon", None, None),
        P("lat", "lon", None, None),
        P("lat", "lon", None, None, None, None),
        P("lat", "lon", None, None, None),
        P("lat", "lon", None, None),
        P("lat", "lon", None, None),
    )
    out_specs = P(None, "lat", "lon", None, None)
    run = functools.partial(per_device, mesh.shape["lat"], mesh.shape["lon"])
    return jax.shard_map(
        run, mesh=mesh, in_specs=in_specs, out_specs=out_specs, check_vma=False
    )
```

```python
import functools

import jax
import jax.numpy as jnp
from jax import lax
from jax.experimental import pallas as pl
from jax.experimental.pallas import tpu as pltpu
from jax.sharding import PartitionSpec as P

VARS = 32
OV = 4
STEPS = 8
PARTS = 2
BLOCK = 128
MESH = pl.DeviceIdType.MESH


def kernel(
    n_lat,
    n_lon,
    lists,
    state,
    reservoir,
    coupling,
    entry,
    read,
    out,
    u0,
    r0,
    r,
    cw,
    iw,
    rw,
    nsw,
    acc,
    send,
    we_in,
    ns_in,
    outbuf,
    send_sem,
    recv_sem,
    load_sem,
    out_sem,
):
    members = u0.shape[0]
    blocks = cw.shape[0]
    links = cw.shape[1] // BLOCK
    pairs = blocks // 2
    own_pairs = [m for m in range(pairs) if m % 3 == 0]
    we_pairs = [m for m in range(pairs) if m % 3 == 1]
    ns_pairs = [m for m in range(pairs) if m % 3 == 2]
    own_blocks = [2 * m + c for m in own_pairs for c in range(2)]
    ns_blocks = [2 * m + c for m in ns_pairs for c in range(2)]

    band = lax.axis_index("lat")
    sector = lax.axis_index("lon")
    east = (band, lax.rem(sector + 1, n_lon))
    west = (band, lax.rem(sector + n_lon - 1, n_lon))
    size = members // PARTS
    far = lax.rem(sector, 2)
    near = 1 - far
    south = (lax.rem(band + 1, n_lat), sector)
    north = (lax.rem(band + n_lat - 1, n_lat), sector)
    has_north = band > 0
    has_south = band < n_lat - 1

    barrier = pltpu.get_barrier_semaphore()
    pl.semaphore_signal(barrier, inc=1, device_id=east, device_id_type=MESH)
    pl.semaphore_signal(barrier, inc=1, device_id=west, device_id_type=MESH)

    @pl.when(has_south)
    def _():
        pl.semaphore_signal(barrier, inc=1, device_id=south, device_id_type=MESH)

    @pl.when(has_north)
    def _():
        pl.semaphore_signal(barrier, inc=1, device_id=north, device_id_type=MESH)

    loads = [
        pltpu.make_async_copy(src, dst, load_sem.at[i])
        for i, (src, dst) in enumerate(
            [(state, u0), (entry, iw), (reservoir, r0), (coupling, cw), (read, rw)]
        )
    ]
    for load in loads:
        load.start()

    def remote(t, src, dst, slot, target):
        return pltpu.make_async_remote_copy(
            src_ref=src,
            dst_ref=dst,
            send_sem=send_sem.at[t, slot],
            recv_sem=recv_sem.at[t, slot],
            device_id=target,
            device_id_type=MESH,
        )

    def to_lon(t, side, part):
        target = (band, lax.rem(sector + 2 * side - 1 + n_lon, n_lon))
        rows = pl.ds(part * size, size)
        return remote(
            t,
            send.at[t, side, rows],
            we_in.at[t, 1 - side, rows],
            2 + (1 - side) * PARTS + part,
            target,
        )

    def to_south(t):
        return remote(t, send.at[t], ns_in.at[t, 0], 0, south)

    def to_north(t):
        return remote(t, send.at[t], ns_in.at[t, 1], 1, north)

    def start_sends(t):
        for part in range(PARTS):
            to_lon(t, near, part).start()

        @pl.when(has_south)
        def _():
            to_south(t).start()

        @pl.when(has_north)
        def _():
            to_north(t).start()

    def wait_sends(t):
        for part in range(PARTS):
            to_lon(t, far, part).wait_send()
            to_lon(t, near, part).wait_send()

        @pl.when(has_south)
        def _():
            to_south(t).wait_send()

        @pl.when(has_north)
        def _():
            to_north(t).wait_send()

    def put_state(t, part, value):
        rounded = value.astype(jnp.bfloat16)
        rows = slice(part * size, (part + 1) * size)
        send[t, 0, rows] = rounded[:, :BLOCK]
        send[t, 1, rows] = rounded[:, BLOCK:]

    def dot(a, b):
        return jnp.dot(a, b, preferred_element_type=jnp.float32)

    loads[0].wait()
    for part in range(PARTS):
        put_state(0, part, u0[part * size : (part + 1) * size, :])
    pl.semaphore_wait(
        barrier, 2 + has_north.astype(jnp.int32) + has_south.astype(jnp.int32)
    )
    for part in range(PARTS):
        to_lon(0, far, part).start()
    start_sends(0)

    @pl.when(jnp.logical_not(has_north))
    def _():
        for t in range(STEPS):
            ns_in[t, 0] = jnp.zeros(ns_in.shape[2:], ns_in.dtype)

    @pl.when(jnp.logical_not(has_south))
    def _():
        for t in range(STEPS):
            ns_in[t, 1] = jnp.zeros(ns_in.shape[2:], ns_in.dtype)

    row = lax.broadcasted_iota(jnp.int32, (2 * BLOCK, BLOCK), 0)
    col = lax.broadcasted_iota(jnp.int32, (2 * BLOCK, BLOCK), 1)
    loads[1].wait()
    for side in range(2):
        target = jnp.full((2 * BLOCK, BLOCK), -VARS, jnp.int32)
        for s in range(OV):
            here = (col >= s * VARS) & (col < (s + 1) * VARS)
            target = jnp.where(here, lists[side, s] * VARS + (col - s * VARS), target)
        onehot = jnp.where(row == target, 1.0, 0.0).astype(jnp.bfloat16)
        for n, m in enumerate(ns_pairs):
            nsw[2 * n + side] = dot(onehot, iw[2 * m + side]).astype(jnp.bfloat16)

    loads[2].wait()
    for b in range(blocks):
        r[b] = r0[:, b * BLOCK : (b + 1) * BLOCK]
    loads[3].wait()
    loads[4].wait()

    def couple(b):
        linked = [r[(b + k) % blocks] for k in range(links)]
        return dot(jnp.concatenate(linked, axis=1), cw[b])

    def finish(indices, activations, rows=slice(None)):
        even = lax.broadcasted_iota(jnp.int32, activations[0].shape, 1) % 2 == 0
        features = []
        for b, activation in zip(indices, activations):
            fresh = jnp.tanh(activation).astype(jnp.bfloat16)
            r[b, rows] = fresh
            wide = fresh.astype(jnp.float32)
            features.append(jnp.where(even, wide * wide, wide).astype(jnp.bfloat16))
        return dot(
            jnp.concatenate(features, axis=1),
            jnp.concatenate([rw[b] for b in indices], axis=0),
        )

    @pl.loop(0, STEPS)
    def _(t):
        own = [send[t, c] for c in range(2)]
        for b in range(blocks):
            total = couple(b)
            if b in own_blocks:
                total += dot(own[b % 2], iw[b])
            acc[b] = total

        result = finish(own_blocks, [acc[b] for b in own_blocks])

        @pl.when(t > 0)
        def _():
            wait_sends(t - 1)
            pltpu.make_async_copy(
                outbuf.at[t - 1], out.at[t - 1], out_sem.at[t - 1]
            ).wait()

        @pl.when(has_north)
        def _():
            to_south(t).wait_recv()

        @pl.when(has_south)
        def _():
            to_north(t).wait_recv()

        sides = [
            jnp.concatenate([ns_in[t, side, 0], ns_in[t, side, 1]], axis=1)
            for side in range(2)
        ]
        result += finish(
            ns_blocks,
            [acc[b] + dot(sides[b % 2], nsw[n]) for n, b in enumerate(ns_blocks)],
        )

        def finish_side(side, rows):
            indices = [2 * m + side for m in we_pairs]
            entered = dot(
                we_in[t, side, rows], jnp.concatenate([iw[b] for b in indices], axis=1)
            )
            activations = [
                acc[b, rows] + entered[:, n * BLOCK : (n + 1) * BLOCK]
                for n, b in enumerate(indices)
            ]
            return finish(indices, activations, rows)

        for part in range(PARTS):
            to_lon(t, 1 - near, part).wait_recv()
        result += finish_side(near, slice(0, members))

        for part in range(PARTS):
            rows = slice(part * size, (part + 1) * size)
            to_lon(t, 1 - far, part).wait_recv()
            value = result[rows] + finish_side(far, rows)

            @pl.when(t < STEPS - 1)
            def _():
                put_state(t + 1, part, value)
                to_lon(t + 1, far, part).start()

            outbuf[t, rows] = value

        @pl.when(t < STEPS - 1)
        def _():
            start_sends(t + 1)

        pltpu.make_async_copy(outbuf.at[t], out.at[t], out_sem.at[t]).start()

    last = STEPS - 1
    wait_sends(last)
    pltpu.make_async_copy(outbuf.at[last], out.at[last], out_sem.at[last]).wait()


def per_device(n_lat, n_lon, initial_state, initial_reservoir, coupling, input_weight, readout, intersection):
    state = initial_state[0, 0]
    reservoir = initial_reservoir[0, 0]
    entry = input_weight[0, 0]
    lists = intersection[0, 0]
    members, features = state.shape
    nodes = reservoir.shape[1]
    blocks, links = coupling.shape[2], coupling.shape[3]
    read = readout[0, 0].reshape(blocks, BLOCK, features)
    weights = coupling[0, 0].reshape(blocks, links * BLOCK, BLOCK)
    ns_count = 2 * len([m for m in range(blocks // 2) if m % 3 == 2])
    hbm = pl.BlockSpec(memory_space=pltpu.MemorySpace.HBM)
    bf16, f32 = jnp.bfloat16, jnp.float32
    forecast = pl.pallas_call(
        functools.partial(kernel, n_lat, n_lon),
        out_shape=jax.ShapeDtypeStruct((STEPS, members, features), f32),
        in_specs=[pl.BlockSpec(memory_space=pltpu.MemorySpace.SMEM)] + [hbm] * 5,
        out_specs=hbm,
        scratch_shapes=[
            pltpu.VMEM((members, features), f32),
            pltpu.VMEM((members, nodes), bf16),
            pltpu.VMEM((blocks, members, BLOCK), bf16),
            pltpu.VMEM((blocks, links * BLOCK, BLOCK), bf16),
            pltpu.VMEM((blocks, BLOCK, BLOCK), bf16),
            pltpu.VMEM((blocks, BLOCK, features), bf16),
            pltpu.VMEM((ns_count, 2 * BLOCK, BLOCK), bf16),
            pltpu.VMEM((blocks, members, BLOCK), f32),
            pltpu.VMEM((STEPS, 2, members, BLOCK), bf16),
            pltpu.VMEM((STEPS, 2, members, BLOCK), bf16),
            pltpu.VMEM((STEPS, 2, 2, members, BLOCK), bf16),
            pltpu.VMEM((STEPS, members, features), f32),
            pltpu.SemaphoreType.DMA((STEPS, 2 + 2 * PARTS)),
            pltpu.SemaphoreType.DMA((STEPS, 2 + 2 * PARTS)),
            pltpu.SemaphoreType.DMA((5,)),
            pltpu.SemaphoreType.DMA((STEPS,)),
        ],
        compiler_params=pltpu.CompilerParams(
            collective_id=0, has_side_effects=True, vmem_limit_bytes=24 * 1024 * 1024
        ),
    )(
        lists,
        *(
            pltpu.with_memory_space_constraint(x, pltpu.MemorySpace.HBM)
            for x in (state, reservoir, weights, entry, read)
        ),
    )
    return forecast[:, None, None]


def solution(mesh):
    in_specs = (
        P("lat", "lon", None, None),
        P("lat", "lon", None, None),
        P("lat", "lon", None, None, None, None),
        P("lat", "lon", None, None, None),
        P("lat", "lon", None, None),
        P("lat", "lon", None, None),
    )
    out_specs = P(None, "lat", "lon", None, None)
    run = functools.partial(per_device, mesh.shape["lat"], mesh.shape["lon"])
    return jax.shard_map(
        run, mesh=mesh, in_specs=in_specs, out_specs=out_specs, check_vma=False
    )
```
